32 devices in a mesh: layer: 1, tok: 32 (over z, y, x, core), qry: 1.
Axes of the slice: x: 2, y: 2, z: 4, core: 2. Of those that a mesh axis runs over, the one named last changes fastest.
Arguments:
- train_grads: bfloat16 [128, 32, 28672], P(('layer', 'tok'), None, 'qry'), may hold values from -6 to 6
- train_acts: bfloat16 [128, 32, 8192], P(('layer', 'tok'), None, 'qry'), may hold values from -6 to 6
- token_index: int32 [128, 32], P('tok'), may hold values from 0 to 31, as said below
- query_grads: bfloat16 [64, 4, 28672], P(('layer', 'tok'), None, 'qry'), may hold values from -6 to 6
- query_acts: bfloat16 [64, 4, 8192], P(('layer', 'tok'), None, 'qry'), may hold values from -6 to 6
- out_basis: bfloat16 [256, 28672], P(('layer', 'tok'), 'qry'), may hold values from -0.03125 to 0.03125
- in_basis: bfloat16 [256, 8192], P(('layer', 'tok'), 'qry'), may hold values from -0.0625 to 0.0625
- corrections: bfloat16 [256, 256], P(('layer', 'tok')), may hold values from 0.099609375 to 10
- damp_table: float32 [80], replicated, may hold values from 0.1 to 1
- layer_id: int32 [1], P('layer'), may hold values from 0 to 79
Outputs:
- token_scores: float32 [128, 32, 64], P(('layer', 'tok', 'qry'))
The draws below stay inside these ranges and needn't reach their ends.
Inputs may be any that keep to these rules, and one draw needn't show every extreme that they name: `token_index`: within one training sequence the 32 indices are distinct.
All inputs are finite; a program needn't handle non-finite values.
Results may differ from the reference program's by a relative error of at most 0.0063.
Values may be sent and summed in bfloat16 or wider, within the bound.
A program may use at most 128 MiB of HBM per device.

```python
import math
import jax
import jax.numpy as jnp
from jax import lax

DIN = 8192
DOUT = 28672
LAYERS = 80
LEN = 32
SEL = 32
QTOK = 4
EIG = 256
NSEQ = 128
NQ = 64


def draw_token_index(key, part):
    key = jax.random.fold_in(key, 11)
    seq_keys = jax.random.split(key, NSEQ)

    def one_sequence(seq_key):
        return jax.random.permutation(seq_key, LEN)[:SEL]
    return jax.vmap(one_sequence)(seq_keys).astype(jnp.int32)


def shard_levels(rng, shape, shards, low, high):
    loudness, own = 1.0, jax.random.fold_in(rng, 6)
    for dim, blocks in shards:
        steps = jnp.exp(jax.random.uniform(jax.random.fold_in(own, dim), (blocks,), jnp.float32, low / len(shards), high / len(shards)))
        loudness = loudness * jnp.repeat(steps, shape[dim] // blocks).reshape([-1 if axis == dim else 1 for axis in range(len(shape))])
    return loudness


def noise(stream_key, dims, width, limit, cuts=(), kind=jnp.bfloat16):
    factor_of = shard_levels(stream_key, dims, cuts, -0.22, 0.18) if cuts else 1.0
    values = jax.random.normal(stream_key, dims, jnp.float32) * width * factor_of
    return jnp.minimum(jnp.maximum(values, -limit), limit).astype(kind)


def setup_inputs(seed: int = 0, part: int = 0) -> dict:
    key_of = jax.random.split(jax.random.key(seed), 11)
    part_splits = jax.random.split(jax.random.fold_in(key_of[10], part), 11)
    return {
        "train_grads": noise(part_splits[0], (NSEQ, LEN, DOUT), 1.0, 6.0, ((0, 32),)),
        "train_acts": noise(part_splits[1], (NSEQ, LEN, DIN), 1.0, 6.0, ((0, 32),)),
        "token_index": draw_token_index(jax.random.fold_in(key_of[10], 71), part),
        "query_grads": noise(part_splits[3], (NQ, QTOK, DOUT), 1.0, 6.0, ((0, 32),)),
        "query_acts": noise(part_splits[4], (NQ, QTOK, DIN), 1.0, 6.0, ((0, 32),)),
        "out_basis": noise(part_splits[5], (EIG, DOUT), DOUT ** -0.5, 0.03125, ((0, 32),)),
        "in_basis": noise(part_splits[6], (EIG, DIN), DIN ** -0.5, 0.0625, ((0, 32),)),
        "corrections": jnp.clip(jnp.exp(math.log(10.0) - 4.609084 * jax.random.uniform(part_splits[7], (EIG, EIG), jnp.float32) ** shard_levels(part_splits[7], (EIG, EIG), ((0, 32),), -0.2, 0.2)), 0.099609375, 10.0).astype(jnp.bfloat16),
        "damp_table": jnp.clip(jnp.exp(jax.random.uniform(key_of[8], (LAYERS,), jnp.float32, math.log(0.1), math.log(1.0))), 0.1, 1.0),
        "layer_id": jax.random.randint(part_splits[9], (1,), 0, LAYERS).astype(jnp.int32),
    }


def pick_positions(values, token_index):

    def pick_sequence(seq_values, seq_index):
        return jnp.take(seq_values, seq_index.astype(jnp.int32), axis=0)
    return jax.vmap(pick_sequence)(values, token_index)

def rotate_rows(row_data, basis):
    flat = row_data.reshape(-1, row_data.shape[-1])
    rotated = jnp.dot(flat, basis.T, preferred_element_type=jnp.float32).astype(jnp.bfloat16)
    return rotated.reshape(row_data.shape[:-1] + (basis.shape[0],))

def reference(train_grads, train_acts, token_index, query_grads, query_acts, out_basis, in_basis, corrections, damp_table, layer_id):
    token_out = rotate_rows(pick_positions(train_grads, token_index), out_basis)
    token_in = rotate_rows(pick_positions(train_acts, token_index), in_basis)
    query_out = rotate_rows(query_grads, out_basis)
    query_in = rotate_rows(query_acts, in_basis)
    chosen = (jnp.arange(LAYERS, dtype=jnp.int32) == layer_id[0]).astype(jnp.float32)
    damping = jnp.sum(damp_table * chosen)
    divisor = corrections.astype(jnp.float32) + damping
    rotated_query = jnp.einsum('qri,qrk->qik', query_out.astype(jnp.float32), query_in.astype(jnp.float32))
    precond_low = (rotated_query / divisor).astype(jnp.bfloat16)
    precond = lax.optimization_barrier(precond_low).astype(jnp.float32)
    score_scale = 1.0 / (EIG * math.sqrt(QTOK))

    def per_sequence(pair):
        seq_out, seq_in = pair
        weighted = jnp.einsum('qik,tk->qti', precond, seq_in.astype(jnp.float32))
        return lax.optimization_barrier(jnp.sum(weighted * seq_out.astype(jnp.float32)[None], axis=2)).T * score_scale
    return lax.map(per_sequence, (token_out, token_in))
```

```python
import math

import jax
import jax.numpy as jnp
from jax import lax
from jax.experimental import pallas as pl
from jax.experimental.pallas import tpu as pltpu
from jax.sharding import PartitionSpec as P

AXES = ("layer", "tok", "qry")
CHIPS = (4, 2, 2)
KINDS = ("zxy",) * 5 + ("yzx",) * 3 + ("xyz",)


def pick_positions(values, token_index):

    def pick_sequence(seq_values, seq_index):
        return jnp.take(seq_values, seq_index, axis=0)

    return jax.vmap(pick_sequence)(values, token_index)


def stack_rows(picked, query_side):
    width = picked.shape[-1]
    return jnp.concatenate([picked.reshape(-1, width), query_side.reshape(-1, width)], axis=0)


def project(row_data, basis_piece):
    return lax.dot_general(
        row_data, basis_piece, (((1,), (1,)), ((), ())), preferred_element_type=jnp.float32
    )


def make_scorer(own_rot, divisor, eigen, query_len, own_count, sel_count):
    score_scale = 1.0 / (eigen * math.sqrt(query_len))
    token_out = own_rot[:, :, :eigen].reshape(-1, eigen)
    token_in = own_rot[:, :, eigen:].reshape(-1, eigen)
    out_values = token_out.astype(jnp.float32)

    def score_query(query_item):
        rotated_query = lax.dot_general(
            query_item[:, :eigen],
            query_item[:, eigen:],
            (((0,), (0,)), ((), ())),
            preferred_element_type=jnp.float32,
        )
        precond = (rotated_query / divisor).astype(jnp.bfloat16)
        weighted = lax.dot_general(
            token_in, precond, (((1,), (1,)), ((), ())), preferred_element_type=jnp.float32
        )
        return jnp.sum(out_values * weighted, axis=1) * score_scale

    def score_block(pieces):
        values = lax.map(score_query, pieces, batch_size=16)
        return values.T.reshape(own_count, sel_count, pieces.shape[0])

    return score_block


def pick_damping(damp_table, layer_id):
    chosen = (jnp.arange(damp_table.shape[0], dtype=jnp.int32) == layer_id[0]).astype(jnp.float32)
    return jnp.sum(damp_table * chosen)


def local(
    train_grads,
    train_acts,
    token_index,
    query_grads,
    query_acts,
    out_basis,
    in_basis,
    corrections,
    damp_table,
    layer_id,
):
    grad_rows = stack_rows(pick_positions(train_grads, token_index), query_grads)
    act_rows = stack_rows(pick_positions(train_acts, token_index), query_acts)
    eigen = corrections.shape[1]
    pieces = (
        lax.all_gather(out_basis, "tok", axis=0, tiled=True),
        lax.all_gather(corrections, "tok", axis=0, tiled=True),
    )
    rot_out = project(grad_rows, pieces[0])
    corr_full = pieces[1]
    rot_in = project(act_rows, lax.all_gather(in_basis, "tok", axis=0, tiled=True))
    rotated = jnp.concatenate([rot_out, rot_in], axis=1)
    seq_count, sel_count = token_index.shape
    query_count, query_len = (query_grads.shape[0], query_grads.shape[1])
    train_part = rotated[: seq_count * sel_count].reshape(seq_count, sel_count, 2 * eigen)
    query_part = rotated[seq_count * sel_count :].reshape(query_count, query_len, 2 * eigen)
    own_count = seq_count // lax.axis_size("qry")
    divisor = corr_full.astype(jnp.float32) + pick_damping(damp_table, layer_id)
    train_sum, query_sum = lax.psum((train_part, query_part), "qry")
    own_train = lax.dynamic_slice_in_dim(train_sum, lax.axis_index("qry") * own_count, own_count, 0)
    scorer = make_scorer(
        own_train.astype(jnp.bfloat16), divisor, eigen, query_len, own_count, sel_count
    )
    return scorer(lax.all_gather(query_sum.astype(jnp.bfloat16), "tok", axis=0, tiled=True))


def rotate_kernel(
    stack_ref,
    grads_ref,
    acts_ref,
    rot_ref,
    query_ref,
    corr_ref,
    basis,
    rows,
    partner,
    acc,
    part_out,
    part_in,
    qpart_out,
    qpart_in,
    queries,
    own_sem,
    pair_send,
    pair_recv,
    up_send,
    down_send,
    z_recv,
    side_send,
    side_recv,
    query_send,
    query_recv,
):
    me = lax.axis_index("tok")
    core = lax.rem(me, 2)
    chip = me // 2
    x = lax.rem(me // 2, 2)
    y = lax.rem(me // 4, 2)
    z = me // 8
    nz = CHIPS[0]
    count = 2 * nz * CHIPS[1] * CHIPS[2]
    sibling = me + 1 - 2 * core
    x_peer = me + 2 - 4 * x
    y_peer = me + 4 - 8 * y
    train, wide_out = grads_ref.shape
    half_out = wide_out // 2
    half_in = acts_ref.shape[1] // 2
    eigen = corr_ref.shape[1]
    chunk = (half_out + half_in) // len(KINDS)
    out_chunks = half_out // chunk

    def span(j):
        extra = eigen if j == len(KINDS) - 1 else 0
        return pl.ds(j * chunk, chunk + extra)

    def remote(src, dst, send, recv, device):
        return pltpu.make_async_remote_copy(
            src_ref=src,
            dst_ref=dst,
            send_sem=send,
            recv_sem=recv,
            device_id=(0, device, 0),
            device_id_type=pl.DeviceIdType.MESH,
        )

    own_copies = [
        pltpu.make_async_copy(
            grads_ref.at[:, pl.ds(core * half_out, half_out)],
            rows.at[pl.ds(0, train), pl.ds(0, half_out)],
            own_sem.at[0],
        ),
        pltpu.make_async_copy(
            acts_ref.at[:, pl.ds(core * half_in, half_in)],
            rows.at[pl.ds(0, train), pl.ds(half_out, half_in)],
            own_sem.at[1],
        ),
    ]
    for copy in own_copies:
        copy.start()

    barrier = pltpu.get_barrier_semaphore()

    def greet(s, carry):
        pl.semaphore_signal(
            barrier,
            inc=1,
            device_id=(0, lax.rem(me + s, count), 0),
            device_id_type=pl.DeviceIdType.MESH,
        )
        return carry

    lax.fori_loop(1, count, greet, 0)
    pl.semaphore_wait(barrier, count - 1)

    stack_copy = remote(stack_ref.at[1 - core], partner, pair_send.at[0], pair_recv.at[0], sibling)
    stack_copy.start()
    row_copies = [
        remote(
            grads_ref.at[:, pl.ds((1 - core) * half_out, half_out)],
            rows.at[pl.ds(train, train), pl.ds(0, half_out)],
            pair_send.at[1],
            pair_recv.at[1],
            sibling,
        ),
        remote(
            acts_ref.at[:, pl.ds((1 - core) * half_in, half_in)],
            rows.at[pl.ds(train, train), pl.ds(half_out, half_in)],
            pair_send.at[2],
            pair_recv.at[2],
            sibling,
        ),
    ]
    for copy in row_copies:
        copy.start()
    acc[...] = jnp.zeros_like(acc)
    stack_copy.wait_recv()

    def build(j):
        cols = span(j)
        own = stack_ref[core, :, cols].astype(jnp.float32)
        other = partner[:, cols].astype(jnp.float32)
        first = jnp.where(core == 0, own, other)
        second = jnp.where(core == 0, other, own)
        basis[y, x, z, :, cols] = jnp.concatenate([first[:8], second[:8]], axis=0).astype(
            jnp.bfloat16
        )
        rows[pl.ds(2 * train, 16), cols] = jnp.concatenate(
            [first[8:], second[8:]], axis=0
        ).astype(jnp.bfloat16)

    def z_block(j, source):
        cols = span(j)
        if KINDS[j] == "zxy":
            return basis.at[y, x, source, :, cols]
        if KINDS[j] == "yzx":
            return basis.at[:, x, source, :, cols]
        return basis.at[:, :, source, :, cols]

    def x_block(j, at_x):
        cols = span(j)
        if KINDS[j] == "zxy":
            return basis.at[y, at_x, :, :, cols]
        if KINDS[j] == "yzx":
            return basis.at[:, at_x, :, :, cols]
        return basis.at[y, at_x, z, :, cols]

    def y_block(j, at_y):
        cols = span(j)
        if KINDS[j] == "zxy":
            return basis.at[at_y, :, :, :, cols]
        if KINDS[j] == "yzx":
            return basis.at[at_y, x, z, :, cols]
        return basis.at[at_y, :, z, :, cols]

    def up_copy(j, source):
        ref = z_block(j, source)
        return remote(ref, ref, up_send.at[j, source], z_recv.at[j, source], me + 8)

    def down_copy(j, source):
        ref = z_block(j, source)
        return remote(ref, ref, down_send.at[j, source], z_recv.at[j, source], me - 8)

    def x_copy(j, at_x):
        ref = x_block(j, at_x)
        return remote(ref, ref, side_send.at[0, j], side_recv.at[0, j], x_peer)

    def y_copy(j, at_y):
        ref = y_block(j, at_y)
        return remote(ref, ref, side_send.at[1, j], side_recv.at[1, j], y_peer)

    def z_start(j):
        @pl.when(z < nz - 1)
        def _():
            up_copy(j, z).start()

        @pl.when(z > 0)
        def _():
            down_copy(j, z).start()

    def z_step(j, s):
        @pl.when(z - s >= 0)
        def _():
            up_copy(j, z - s).wait_recv()

            @pl.when(z < nz - 1)
            def _():
                up_copy(j, z - s).start()

        @pl.when(z + s < nz)
        def _():
            down_copy(j, z + s).wait_recv()

            @pl.when(z > 0)
            def _():
                down_copy(j, z + s).start()

    def x_start(j):
        x_copy(j, x).start()

    def y_start(j):
        y_copy(j, y).start()

    def x_wait(j):
        x_copy(j, 1 - x).wait_recv()

    def y_wait(j):
        y_copy(j, 1 - y).wait_recv()

    def natural(cols):
        return jnp.concatenate(
            [
                basis[b, a, c, :, cols]
                for c in range(nz)
                for b in range(CHIPS[1])
                for a in range(CHIPS[2])
            ],
            axis=0,
        )

    def compute(j):
        side = 0 if j < out_chunks else 1
        cols = pl.ds(j * chunk, chunk)
        acc[side] += lax.dot_general(
            rows[:, cols],
            natural(cols),
            (((1,), (1,)), ((), ())),
            preferred_element_type=jnp.float32,
        )

    last = len(KINDS) - 1
    for j in (0, 5, 8, 1, 6, 2, 7, 3, 4):
        build(j)
        {"z": z_start, "x": x_start, "y": y_start}[KINDS[j][0]](j)
    for j in (0, 1, 2):
        z_step(j, 1)
    x_wait(8)
    y_start(8)
    for j in (0, 1, 2):
        z_step(j, 2)
    for j in (0, 1, 2):
        z_step(j, 3)
        x_start(j)
    y_wait(5)
    z_start(5)
    z_step(3, 1)
    z_step(4, 1)
    x_wait(0)
    y_start(0)
    z_step(5, 1)
    z_step(3, 2)
    z_step(4, 2)
    y_wait(6)
    z_start(6)
    x_wait(1)
    y_start(1)
    z_step(5, 2)
    z_step(3, 3)
    x_start(3)
    x_wait(2)
    y_start(2)
    z_step(5, 3)
    x_start(5)
    z_step(4, 3)
    x_start(4)
    z_step(6, 1)
    y_wait(7)
    z_start(7)
    for copy in own_copies:
        copy.wait()
    for copy in row_copies:
        copy.wait_recv()
    y_wait(0)
    compute(0)
    z_step(6, 2)
    x_wait(3)
    y_start(3)
    z_step(6, 3)
    x_start(6)
    y_wait(8)
    z_start(8)
    z_step(7, 1)
    x_wait(4)
    y_start(4)
    y_wait(1)
    compute(1)
    z_step(7, 2)
    x_wait(5)
    compute(5)
    z_step(8, 1)
    z_step(7, 3)
    x_start(7)
    y_wait(2)
    compute(2)
    z_step(8, 2)
    y_wait(3)
    compute(3)
    x_wait(6)
    compute(6)
    z_step(8, 3)
    compute(8)
    y_wait(4)
    compute(4)
    x_wait(7)
    compute(7)

    qpart_out[...] = acc[1 - core, pl.ds(2 * train, 16), :]
    qpart_copy = remote(qpart_out, qpart_in, pair_send.at[3], pair_recv.at[3], sibling)
    qpart_copy.start()
    part_out[...] = acc[:, pl.ds(train, train), :]
    part_copy = remote(part_out, part_in, pair_send.at[4], pair_recv.at[4], sibling)
    part_copy.start()
    qpart_copy.wait_recv()
    queries[core, chip] = (acc[core, pl.ds(2 * train, 16), :] + qpart_in[...]).astype(jnp.bfloat16)

    def query_copy(source, target):
        ref = queries.at[lax.rem(source, 2), source // 2]
        return remote(ref, ref, query_send.at[target], query_recv.at[source], target)

    def send_query(s, carry):
        query_copy(me, lax.rem(me + s, count)).start()
        return carry

    lax.fori_loop(1, count, send_query, 0)
    corr_ref[...] = natural(pl.ds(half_out + half_in, eigen))
    part_copy.wait_recv()
    rot_ref[...] = (acc[:, pl.ds(0, train), :] + part_in[...]).astype(jnp.bfloat16)

    def wait_query(s, carry):
        source = lax.rem(me + s, count)
        query_copy(source, source).wait_recv()
        return carry

    lax.fori_loop(1, count, wait_query, 0)
    query_ref[...] = queries[...].reshape(query_ref.shape)

    stack_copy.wait_send()
    for copy in row_copies:
        copy.wait_send()
    qpart_copy.wait_send()
    part_copy.wait_send()
    for j in range(last + 1):
        x_copy(j, x).wait_send()
        y_copy(j, y).wait_send()
        for s in range(nz):

            @pl.when(jnp.logical_and(z < nz - 1, z - s >= 0))
            def _():
                up_copy(j, z - s).wait_send()

            @pl.when(jnp.logical_and(z > 0, z + s < nz))
            def _():
                down_copy(j, z + s).wait_send()

    def finish_query(s, carry):
        query_copy(me, lax.rem(me + s, count)).wait_send()
        return carry

    lax.fori_loop(1, count, finish_query, 0)


def rotate_all(stack, grads, acts, eigen):
    train, wide = grads.shape
    total = stack.shape[2]
    nz, ny, nx = CHIPS
    chips = nz * ny * nx
    n = len(KINDS)
    dma = pltpu.SemaphoreType.DMA
    vmem = pl.BlockSpec(memory_space=pltpu.VMEM)
    hbm = pl.BlockSpec(memory_space=pl.ANY)
    return pl.pallas_call(
        rotate_kernel,
        out_shape=(
            jax.ShapeDtypeStruct((2, train, eigen), jnp.bfloat16),
            jax.ShapeDtypeStruct((2, chips * 16, eigen), jnp.bfloat16),
            jax.ShapeDtypeStruct((eigen, eigen), jnp.bfloat16),
        ),
        in_specs=[vmem, hbm, hbm],
        out_specs=(vmem, vmem, vmem),
        scratch_shapes=[
            pltpu.VMEM((ny, nx, nz, 16, total), jnp.bfloat16),
            pltpu.VMEM((2 * train + 16, total), jnp.bfloat16),
            pltpu.VMEM((16, total), jnp.bfloat16),
            pltpu.VMEM((2, 2 * train + 16, eigen), jnp.float32),
            pltpu.VMEM((2, train, eigen), jnp.float32),
            pltpu.VMEM((2, train, eigen), jnp.float32),
            pltpu.VMEM((16, eigen), jnp.float32),
            pltpu.VMEM((16, eigen), jnp.float32),
            pltpu.VMEM((2, chips, 16, eigen), jnp.bfloat16),
            dma((2,)),
            dma((5,)),
            dma((5,)),
            dma((n, nz)),
            dma((n, nz)),
            dma((n, nz)),
            dma((2, n)),
            dma((2, n)),
            dma((2 * chips,)),
            dma((2 * chips,)),
        ],
        compiler_params=pltpu.CompilerParams(
            collective_id=0, has_side_effects=True, vmem_limit_bytes=44 * 1024 * 1024
        ),
        cost_estimate=pl.CostEstimate(
            flops=4 * train * total * eigen, bytes_accessed=4 * train * wide, transcendentals=0
        ),
    )(stack, grads, acts)


def local_fused(
    train_grads,
    train_acts,
    token_index,
    query_grads,
    query_acts,
    out_basis,
    in_basis,
    corrections,
    damp_table,
    layer_id,
):
    eigen = corrections.shape[1]
    seq_count, sel_count = token_index.shape
    length = train_grads.shape[1]
    query_count, query_len = query_grads.shape[:2]
    rows_q = query_count * query_len
    wide_out, wide_in = out_basis.shape[1], in_basis.shape[1]
    out_rows = jnp.concatenate([out_basis, query_grads.reshape(rows_q, wide_out)], axis=0)
    in_rows = jnp.concatenate([in_basis, query_acts.reshape(rows_q, wide_in)], axis=0)
    corr_rows = jnp.concatenate([corrections, jnp.zeros((rows_q, eigen), corrections.dtype)], axis=0)
    stack = jnp.stack(
        [
            jnp.concatenate(
                [
                    out_rows[:, h * (wide_out // 2) : (h + 1) * (wide_out // 2)],
                    in_rows[:, h * (wide_in // 2) : (h + 1) * (wide_in // 2)],
                    corr_rows,
                ],
                axis=1,
            )
            for h in range(2)
        ],
        axis=0,
    )
    rot, queries, corr = rotate_all(
        stack,
        train_grads.reshape(-1, wide_out),
        train_acts.reshape(-1, wide_in),
        eigen,
    )
    one_hot = (token_index[:, :, None] == jnp.arange(length, dtype=token_index.dtype)).astype(
        jnp.bfloat16
    )
    positions = jnp.concatenate([rot[0], rot[1]], axis=1).reshape(seq_count, length, 2 * eigen)
    own_rot = jnp.einsum(
        "sjl,sle->sje", one_hot, positions, preferred_element_type=jnp.float32
    ).astype(jnp.bfloat16)
    divisor = corr.astype(jnp.float32) + pick_damping(damp_table, layer_id)
    scorer = make_scorer(own_rot, divisor, eigen, query_len, seq_count, sel_count)
    pieces = jnp.concatenate([queries[0], queries[1]], axis=1)
    return scorer(pieces.reshape(-1, query_len, 2 * eigen))


def solution(mesh):
    in_specs = (
        P(("layer", "tok"), None, "qry"),
        P(("layer", "tok"), None, "qry"),
        P("tok", None),
        P(("layer", "tok"), None, "qry"),
        P(("layer", "tok"), None, "qry"),
        P(("layer", "tok"), "qry"),
        P(("layer", "tok"), "qry"),
        P(("layer", "tok"), None),
        P(),
        P("layer"),
    )
    out_specs = P(("layer", "tok", "qry"), None, None)
    sizes = tuple(mesh.shape[axis] for axis in AXES)
    fused = sizes == (1, 2 * CHIPS[0] * CHIPS[1] * CHIPS[2], 1)
    return jax.shard_map(
        local_fused if fused else local,
        mesh=mesh,
        in_specs=in_specs,
        out_specs=out_specs,
        check_vma=False,
    )
```

```python
import math

import jax
import jax.numpy as jnp
from jax import lax
from jax.experimental import pallas as pl
from jax.experimental.pallas import tpu as pltpu
from jax.sharding import PartitionSpec as P

AXES = ("layer", "tok", "qry")
CHIPS = (4, 2, 2)
EARLY = 3
KINDS = (
    "zyx",
    "zxy",
    "zxy",
    "xyz",
    "yzx",
    "zxy",
    "zyx",
    "xyz",
    "zyx",
    "zyx",
    "xzy",
    "zxy",
    "yxz",
    "yxz",
    "zyx",
    "zxy",
    "zxy",
    "zyx",
)
ORDER = (
    (0, -1, 0), (1, -1, 0), (2, -1, 0), (0, 0, 1), (1, 0, 1), (2, 0, 1),
    (0, 0, 2), (3, -1, 0), (4, -1, 0), (1, 0, 2), (5, -1, 0), (2, 0, 2),
    (3, 0, 1), (6, -1, 0), (7, -1, 0), (0, 0, 3), (1, 0, 3), (5, 0, 1),
    (2, 0, 3), (4, 0, 1), (6, 0, 1), (5, 0, 2), (3, 1, 1), (6, 0, 2),
    (8, -1, 0), (1, 1, 1), (5, 0, 3), (0, 1, 1), (7, 0, 1), (4, 1, 1),
    (6, 0, 3), (2, 1, 1), (9, -1, 0), (10, -1, 0), (3, 2, 1), (8, 0, 1),
    (4, 1, 2), (1, 2, 1), (1, 9, 0), (4, 1, 3), (11, -1, 0), (9, 0, 1),
    (5, 1, 1), (6, 1, 1), (0, 2, 1), (0, 9, 0), (3, 2, 2), (8, 0, 2),
    (7, 1, 1), (3, 2, 3), (3, 9, 0), (2, 2, 1), (2, 9, 0), (10, 0, 1),
    (8, 0, 3), (11, 0, 1), (4, 2, 1), (4, 9, 0), (12, -1, 0), (9, 0, 2),
    (9, 0, 3), (11, 0, 2), (11, 0, 3), (13, -1, 0), (7, 2, 1), (5, 2, 1),
    (6, 2, 1), (5, 9, 0), (6, 9, 0), (14, -1, 0), (10, 1, 1), (8, 1, 1),
    (15, -1, 0), (16, -1, 0), (11, 1, 1), (12, 0, 1), (7, 2, 2), (9, 1, 1),
    (13, 0, 1), (17, -1, 0), (7, 2, 3), (7, 9, 0), (10, 1, 2), (8, 2, 1),
    (8, 9, 0), (14, 0, 1), (10, 1, 3), (14, 0, 2), (15, 0, 1), (16, 0, 1),
    (14, 0, 3), (15, 0, 2), (12, 1, 1), (16, 0, 2), (17, 0, 1), (9, 2, 1),
    (11, 2, 1), (9, 9, 0), (11, 9, 0), (15, 0, 3), (16, 0, 3), (10, 2, 1),
    (13, 1, 1), (10, 9, 0), (17, 0, 2), (17, 0, 3), (14, 1, 1), (15, 1, 1),
    (12, 2, 1), (16, 1, 1), (17, 1, 1), (13, 2, 1), (12, 2, 2), (14, 2, 1),
    (15, 2, 1), (14, 9, 0), (15, 9, 0), (12, 2, 3), (12, 9, 0), (13, 2, 2),
    (16, 2, 1), (17, 2, 1), (16, 9, 0), (17, 9, 0), (13, 2, 3), (13, 9, 0),
)


def pick_positions(values, token_index):

    def pick_sequence(seq_values, seq_index):
        return jnp.take(seq_values, seq_index, axis=0)

    return jax.vmap(pick_sequence)(values, token_index)


def stack_rows(picked, query_side):
    width = picked.shape[-1]
    return jnp.concatenate([picked.reshape(-1, width), query_side.reshape(-1, width)], axis=0)


def project(row_data, basis_piece):
    return lax.dot_general(
        row_data, basis_piece, (((1,), (1,)), ((), ())), preferred_element_type=jnp.float32
    )


def make_scorer(own_rot, divisor, eigen, query_len, own_count, sel_count):
    score_scale = 1.0 / (eigen * math.sqrt(query_len))
    token_out = own_rot[:, :, :eigen].reshape(-1, eigen)
    token_in = own_rot[:, :, eigen:].reshape(-1, eigen)
    out_values = token_out.astype(jnp.float32)

    def score_query(query_item):
        rotated_query = lax.dot_general(
            query_item[:, :eigen],
            query_item[:, eigen:],
            (((0,), (0,)), ((), ())),
            preferred_element_type=jnp.float32,
        )
        precond = (rotated_query / divisor).astype(jnp.bfloat16)
        weighted = lax.dot_general(
            token_in, precond, (((1,), (1,)), ((), ())), preferred_element_type=jnp.float32
        )
        return jnp.sum(out_values * weighted, axis=1) * score_scale

    def score_block(pieces):
        values = lax.map(score_query, pieces, batch_size=16)
        return values.T.reshape(own_count, sel_count, pieces.shape[0])

    return score_block


def pick_damping(damp_table, layer_id):
    chosen = (jnp.arange(damp_table.shape[0], dtype=jnp.int32) == layer_id[0]).astype(jnp.float32)
    return jnp.sum(damp_table * chosen)


def local(
    train_grads,
    train_acts,
    token_index,
    query_grads,
    query_acts,
    out_basis,
    in_basis,
    corrections,
    damp_table,
    layer_id,
):
    grad_rows = stack_rows(pick_positions(train_grads, token_index), query_grads)
    act_rows = stack_rows(pick_positions(train_acts, token_index), query_acts)
    eigen = corrections.shape[1]
    pieces = (
        lax.all_gather(out_basis, "tok", axis=0, tiled=True),
        lax.all_gather(corrections, "tok", axis=0, tiled=True),
    )
    rot_out = project(grad_rows, pieces[0])
    corr_full = pieces[1]
    rot_in = project(act_rows, lax.all_gather(in_basis, "tok", axis=0, tiled=True))
    rotated = jnp.concatenate([rot_out, rot_in], axis=1)
    seq_count, sel_count = token_index.shape
    query_count, query_len = (query_grads.shape[0], query_grads.shape[1])
    train_part = rotated[: seq_count * sel_count].reshape(seq_count, sel_count, 2 * eigen)
    query_part = rotated[seq_count * sel_count :].reshape(query_count, query_len, 2 * eigen)
    own_count = seq_count // lax.axis_size("qry")
    divisor = corr_full.astype(jnp.float32) + pick_damping(damp_table, layer_id)
    train_sum, query_sum = lax.psum((train_part, query_part), "qry")
    own_train = lax.dynamic_slice_in_dim(train_sum, lax.axis_index("qry") * own_count, own_count, 0)
    scorer = make_scorer(
        own_train.astype(jnp.bfloat16), divisor, eigen, query_len, own_count, sel_count
    )
    return scorer(lax.all_gather(query_sum.astype(jnp.bfloat16), "tok", axis=0, tiled=True))


def rotate_kernel(
    out_ref,
    in_ref,
    own_corr_ref,
    query_grads_ref,
    query_acts_ref,
    grads_ref,
    acts_ref,
    rot_ref,
    query_ref,
    corr_ref,
    stack_ref,
    basis,
    rows,
    partner,
    acc,
    part_out,
    part_in,
    qpart_out,
    qpart_in,
    queries,
    own_sem,
    pair_send,
    pair_recv,
    up_send,
    down_send,
    z_recv,
    side_send,
    side_recv,
    query_send,
    query_recv,
):
    me = lax.axis_index("tok")
    core = lax.rem(me, 2)
    chip = me // 2
    x = lax.rem(me // 2, 2)
    y = lax.rem(me // 4, 2)
    z = me // 8
    nz = CHIPS[0]
    count = 2 * nz * CHIPS[1] * CHIPS[2]
    sibling = me + 1 - 2 * core
    x_peer = me + 2 - 4 * x
    y_peer = me + 4 - 8 * y
    train, wide_out = grads_ref.shape
    half_out = wide_out // 2
    half_in = acts_ref.shape[1] // 2
    eigen = corr_ref.shape[1]
    chunk = (half_out + half_in) // len(KINDS)
    out_chunks = half_out // chunk

    def span(j):
        extra = eigen if j == len(KINDS) - 1 else 0
        return pl.ds(j * chunk, chunk + extra)

    def remote(src, dst, send, recv, device):
        return pltpu.make_async_remote_copy(
            src_ref=src,
            dst_ref=dst,
            send_sem=send,
            recv_sem=recv,
            device_id=(0, device, 0),
            device_id_type=pl.DeviceIdType.MESH,
        )

    own_copies = [
        pltpu.make_async_copy(
            grads_ref.at[:, pl.ds(core * half_out, half_out)],
            rows.at[pl.ds(0, train), pl.ds(0, half_out)],
            own_sem.at[0],
        ),
        pltpu.make_async_copy(
            acts_ref.at[:, pl.ds(core * half_in, half_in)],
            rows.at[pl.ds(0, train), pl.ds(half_out, half_in)],
            own_sem.at[1],
        ),
    ]
    for copy in own_copies:
        copy.start()

    barrier = pltpu.get_barrier_semaphore()

    def greet(s, carry):
        pl.semaphore_signal(
            barrier,
            inc=1,
            device_id=(0, lax.rem(me + s, count), 0),
            device_id_type=pl.DeviceIdType.MESH,
        )
        return carry

    lax.fori_loop(1, count, greet, 0)

    def pack(half, at, own, query, source, width):
        tops = own[:, pl.ds(source, width)].astype(jnp.float32)
        if query is None:
            ends = [jnp.zeros((8, width), jnp.float32)]
        else:
            ends = [
                query[q, :, pl.ds(source, width)].astype(jnp.float32)
                for q in range(query.shape[0])
            ]
        stack_ref[half, :, pl.ds(at, width)] = jnp.concatenate([tops, *ends], axis=0).astype(
            jnp.bfloat16
        )

    for half in range(2):
        for at in range(0, half_out, chunk):
            pack(half, at, out_ref, query_grads_ref, half * half_out + at, chunk)
        for at in range(0, half_in, chunk):
            pack(half, half_out + at, in_ref, query_acts_ref, half * half_in + at, chunk)
        pack(half, half_out + half_in, own_corr_ref, None, 0, eigen)
    pl.semaphore_wait(barrier, count - 1)

    early = EARLY * chunk
    stack_copies = [
        remote(
            stack_ref.at[1 - core, :, cols],
            partner.at[:, cols],
            pair_send.at[slot],
            pair_recv.at[slot],
            sibling,
        )
        for slot, cols in ((0, pl.ds(0, early)), (5, pl.ds(early, partner.shape[1] - early)))
    ]
    for copy in stack_copies:
        copy.start()
    row_copies = [
        remote(
            grads_ref.at[:, pl.ds((1 - core) * half_out, half_out)],
            rows.at[pl.ds(train, train), pl.ds(0, half_out)],
            pair_send.at[1],
            pair_recv.at[1],
            sibling,
        ),
        remote(
            acts_ref.at[:, pl.ds((1 - core) * half_in, half_in)],
            rows.at[pl.ds(train, train), pl.ds(half_out, half_in)],
            pair_send.at[2],
            pair_recv.at[2],
            sibling,
        ),
    ]
    for copy in row_copies:
        copy.start()
    acc[...] = jnp.zeros_like(acc)

    def build(j):
        cols = span(j)
        own = stack_ref[core, :, cols].astype(jnp.float32)
        other = partner[:, cols].astype(jnp.float32)
        first = jnp.where(core == 0, own, other)
        second = jnp.where(core == 0, other, own)
        basis[y, x, z, :, cols] = jnp.concatenate([first[:8], second[:8]], axis=0).astype(
            jnp.bfloat16
        )
        rows[pl.ds(2 * train, 16), cols] = jnp.concatenate(
            [first[8:], second[8:]], axis=0
        ).astype(jnp.bfloat16)

    def block(j, axis, at):
        before = KINDS[j][: KINDS[j].index(axis)]
        place = {"y": y, "x": x, "z": z, axis: at}
        index = [slice(None) if a in before else place[a] for a in "yxz"]
        return basis.at[(*index, slice(None), span(j))]

    def up_copy(j, source):
        ref = block(j, "z", source)
        return remote(ref, ref, up_send.at[j, source], z_recv.at[j, source], me + 8)

    def down_copy(j, source):
        ref = block(j, "z", source)
        return remote(ref, ref, down_send.at[j, source], z_recv.at[j, source], me - 8)

    def x_copy(j, at_x):
        ref = block(j, "x", at_x)
        return remote(ref, ref, side_send.at[0, j], side_recv.at[0, j], x_peer)

    def y_copy(j, at_y):
        ref = block(j, "y", at_y)
        return remote(ref, ref, side_send.at[1, j], side_recv.at[1, j], y_peer)

    def z_start(j):
        @pl.when(z < nz - 1)
        def _():
            up_copy(j, z).start()

        @pl.when(z > 0)
        def _():
            down_copy(j, z).start()

    def z_step(j, s):
        @pl.when(z - s >= 0)
        def _():
            up_copy(j, z - s).wait_recv()

            @pl.when(z < nz - 1)
            def _():
                up_copy(j, z - s).start()

        @pl.when(z + s < nz)
        def _():
            down_copy(j, z + s).wait_recv()

            @pl.when(z > 0)
            def _():
                down_copy(j, z + s).start()

    def x_start(j):
        x_copy(j, x).start()

    def y_start(j):
        y_copy(j, y).start()

    def x_wait(j):
        x_copy(j, 1 - x).wait_recv()

    def y_wait(j):
        y_copy(j, 1 - y).wait_recv()

    def natural(cols):
        return jnp.concatenate(
            [
                basis[b, a, c, :, cols]
                for c in range(nz)
                for b in range(CHIPS[1])
                for a in range(CHIPS[2])
            ],
            axis=0,
        )

    def compute(j):
        side = 0 if j < out_chunks else 1
        cols = pl.ds(j * chunk, chunk)
        acc[side] += lax.dot_general(
            rows[:, cols],
            natural(cols),
            (((1,), (1,)), ((), ())),
            preferred_element_type=jnp.float32,
        )

    last = len(KINDS) - 1
    starts = {"z": z_start, "x": x_start, "y": y_start}
    rows_here = False
    for j, place, step in ORDER:
        if place < 0:
            if j in (0, EARLY):
                stack_copies[j // EARLY].wait_recv()
            build(j)
            starts[KINDS[j][0]](j)
        elif place < len(KINDS[j]):
            axis = KINDS[j][place]
            if axis == "z":
                z_step(j, step)
            else:
                {"x": x_wait, "y": y_wait}[axis](j)
            if place + 1 < len(KINDS[j]) and (axis != "z" or step == nz - 1):
                starts[KINDS[j][place + 1]](j)
        else:
            if not rows_here:
                rows_here = True
                for copy in own_copies:
                    copy.wait()
                for copy in row_copies:
                    copy.wait_recv()
            compute(j)

    qpart_out[...] = acc[1 - core, pl.ds(2 * train, 16), :]
    qpart_copy = remote(qpart_out, qpart_in, pair_send.at[3], pair_recv.at[3], sibling)
    qpart_copy.start()
    part_out[...] = acc[:, pl.ds(train, train), :]
    part_copy = remote(part_out, part_in, pair_send.at[4], pair_recv.at[4], sibling)
    part_copy.start()
    qpart_copy.wait_recv()
    queries[core, chip] = (acc[core, pl.ds(2 * train, 16), :] + qpart_in[...]).astype(jnp.bfloat16)

    def query_copy(source, target):
        ref = queries.at[lax.rem(source, 2), source // 2]
        return remote(ref, ref, query_send.at[target], query_recv.at[source], target)

    def send_query(s, carry):
        query_copy(me, lax.rem(me + s, count)).start()
        return carry

    lax.fori_loop(1, count, send_query, 0)
    corr_ref[...] = natural(pl.ds(half_out + half_in, eigen))
    part_copy.wait_recv()
    rot_ref[...] = (acc[:, pl.ds(0, train), :] + part_in[...]).astype(jnp.bfloat16)

    for copy in stack_copies + row_copies:
        copy.wait_send()
    qpart_copy.wait_send()
    part_copy.wait_send()
    for j in range(last + 1):
        x_copy(j, x).wait_send()
        y_copy(j, y).wait_send()
        for s in range(nz):

            @pl.when(jnp.logical_and(z < nz - 1, z - s >= 0))
            def _():
                up_copy(j, z - s).wait_send()

            @pl.when(jnp.logical_and(z > 0, z + s < nz))
            def _():
                down_copy(j, z + s).wait_send()

    def wait_query(s, carry):
        source = lax.rem(me + s, count)
        query_copy(source, source).wait_recv()
        return carry

    lax.fori_loop(1, count, wait_query, 0)
    query_ref[...] = queries[...].reshape(query_ref.shape)

    def finish_query(s, carry):
        query_copy(me, lax.rem(me + s, count)).wait_send()
        return carry

    lax.fori_loop(1, count, finish_query, 0)


def rotate_all(out_basis, in_basis, corrections, query_grads, query_acts, grads, acts):
    train, wide = grads.shape
    eigen = corrections.shape[1]
    total = (wide + acts.shape[1]) // 2 + eigen
    nz, ny, nx = CHIPS
    chips = nz * ny * nx
    n = len(KINDS)
    dma = pltpu.SemaphoreType.DMA
    vmem = pl.BlockSpec(memory_space=pltpu.VMEM)
    hbm = pl.BlockSpec(memory_space=pltpu.HBM)
    return pl.pallas_call(
        rotate_kernel,
        out_shape=(
            jax.ShapeDtypeStruct((2, train, eigen), jnp.bfloat16),
            jax.ShapeDtypeStruct((2, chips * 16, eigen), jnp.bfloat16),
            jax.ShapeDtypeStruct((eigen, eigen), jnp.bfloat16),
        ),
        in_specs=[vmem] * 5 + [hbm] * 2,
        out_specs=(vmem, vmem, vmem),
        scratch_shapes=[
            pltpu.VMEM((2, 16, total), jnp.bfloat16),
            pltpu.VMEM((ny, nx, nz, 16, total), jnp.bfloat16),
            pltpu.VMEM((2 * train + 16, total), jnp.bfloat16),
            pltpu.VMEM((16, total), jnp.bfloat16),
            pltpu.VMEM((2, 2 * train + 16, eigen), jnp.float32),
            pltpu.VMEM((2, train, eigen), jnp.float32),
            pltpu.VMEM((2, train, eigen), jnp.float32),
            pltpu.VMEM((16, eigen), jnp.float32),
            pltpu.VMEM((16, eigen), jnp.float32),
            pltpu.VMEM((2, chips, 16, eigen), jnp.bfloat16),
            dma((2,)),
            dma((6,)),
            dma((6,)),
            dma((n, nz)),
            dma((n, nz)),
            dma((n, nz)),
            dma((2, n)),
            dma((2, n)),
            dma((2 * chips,)),
            dma((2 * chips,)),
        ],
        compiler_params=pltpu.CompilerParams(
            collective_id=0, has_side_effects=True, vmem_limit_bytes=53 * 1024 * 1024
        ),
        cost_estimate=pl.CostEstimate(
            flops=4 * train * total * eigen, bytes_accessed=4 * train * wide, transcendentals=0
        ),
    )(out_basis, in_basis, corrections, query_grads, query_acts, grads, acts)


def local_fused(
    train_grads,
    train_acts,
    token_index,
    query_grads,
    query_acts,
    out_basis,
    in_basis,
    corrections,
    damp_table,
    layer_id,
):
    eigen = corrections.shape[1]
    seq_count, sel_count = token_index.shape
    length = train_grads.shape[1]
    query_len = query_grads.shape[1]
    wide_out, wide_in = out_basis.shape[1], in_basis.shape[1]
    rot, queries, corr = rotate_all(
        out_basis,
        in_basis,
        corrections,
        query_grads,
        query_acts,
        train_grads.reshape(-1, wide_out),
        train_acts.reshape(-1, wide_in),
    )
    one_hot = (token_index[:, :, None] == jnp.arange(length, dtype=token_index.dtype)).astype(
        jnp.bfloat16
    )
    positions = jnp.concatenate([rot[0], rot[1]], axis=1).reshape(seq_count, length, 2 * eigen)
    own_rot = jnp.einsum(
        "sjl,sle->sje", one_hot, positions, preferred_element_type=jnp.float32
    ).astype(jnp.bfloat16)
    divisor = corr.astype(jnp.float32) + pick_damping(damp_table, layer_id)
    scorer = make_scorer(own_rot, divisor, eigen, query_len, seq_count, sel_count)
    pieces = jnp.concatenate([queries[0], queries[1]], axis=1)
    return scorer(pieces.reshape(-1, query_len, 2 * eigen))


def solution(mesh):
    in_specs = (
        P(("layer", "tok"), None, "qry"),
        P(("layer", "tok"), None, "qry"),
        P("tok", None),
        P(("layer", "tok"), None, "qry"),
        P(("layer", "tok"), None, "qry"),
        P(("layer", "tok"), "qry"),
        P(("layer", "tok"), "qry"),
        P(("layer", "tok"), None),
        P(),
        P("layer"),
    )
    out_specs = P(("layer", "tok", "qry"), None, None)
    sizes = tuple(mesh.shape[axis] for axis in AXES)
    fused = sizes == (1, 2 * CHIPS[0] * CHIPS[1] * CHIPS[2], 1)
    return jax.shard_map(
        local_fused if fused else local,
        mesh=mesh,
        in_specs=in_specs,
        out_specs=out_specs,
        check_vma=False,
    )
```

```python
import math

import jax
import jax.numpy as jnp
from jax import lax
from jax.experimental import pallas as pl
from jax.experimental.pallas import tpu as pltpu
from jax.sharding import PartitionSpec as P

AXES = ("layer", "tok", "qry")
CHIPS = (4, 2, 2)
EARLY = 3
KINDS = (
    "zyx",
    "zxy",
    "zxy",
    "xyz",
    "yzx",
    "zxy",
    "zyx",
    "xyz",
    "zyx",
    "zyx",
    "xzy",
    "zxy",
    "yxz",
    "yxz",
    "zyx",
    "zxy",
    "zxy",
    "zyx",
)
ORDER = (
    (0, -1, 0), (1, -1, 0), (2, -1, 0), (0, 0, 1), (1, 0, 1), (2, 0, 1),
    (0, 0, 2), (3, -1, 0), (4, -1, 0), (1, 0, 2), (5, -1, 0), (2, 0, 2),
    (3, 0, 1), (6, -1, 0), (7, -1, 0), (0, 0, 3), (1, 0, 3), (5, 0, 1),
    (2, 0, 3), (4, 0, 1), (6, 0, 1), (5, 0, 2), (3, 1, 1), (6, 0, 2),
    (8, -1, 0), (1, 1, 1), (5, 0, 3), (0, 1, 1), (7, 0, 1), (4, 1, 1),
    (6, 0, 3), (2, 1, 1), (9, -1, 0), (10, -1, 0), (3, 2, 1), (8, 0, 1),
    (4, 1, 2), (1, 2, 1), (1, 9, 0), (4, 1, 3), (11, -1, 0), (9, 0, 1),
    (5, 1, 1), (6, 1, 1), (0, 2, 1), (0, 9, 0), (3, 2, 2), (8, 0, 2),
    (7, 1, 1), (3, 2, 3), (3, 9, 0), (2, 2, 1), (2, 9, 0), (10, 0, 1),
    (8, 0, 3), (11, 0, 1), (4, 2, 1), (4, 9, 0), (12, -1, 0), (9, 0, 2),
    (9, 0, 3), (11, 0, 2), (11, 0, 3), (13, -1, 0), (7, 2, 1), (5, 2, 1),
    (6, 2, 1), (5, 9, 0), (6, 9, 0), (14, -1, 0), (10, 1, 1), (8, 1, 1),
    (15, -1, 0), (16, -1, 0), (11, 1, 1), (12, 0, 1), (7, 2, 2), (9, 1, 1),
    (13, 0, 1), (17, -1, 0), (7, 2, 3), (7, 9, 0), (10, 1, 2), (8, 2, 1),
    (8, 9, 0), (14, 0, 1), (10, 1, 3), (14, 0, 2), (15, 0, 1), (16, 0, 1),
    (14, 0, 3), (15, 0, 2), (12, 1, 1), (16, 0, 2), (17, 0, 1), (9, 2, 1),
    (11, 2, 1), (9, 9, 0), (11, 9, 0), (15, 0, 3), (16, 0, 3), (10, 2, 1),
    (13, 1, 1), (10, 9, 0), (17, 0, 2), (17, 0, 3), (14, 1, 1), (15, 1, 1),
    (12, 2, 1), (16, 1, 1), (17, 1, 1), (13, 2, 1), (12, 2, 2), (14, 2, 1),
    (15, 2, 1), (14, 9, 0), (15, 9, 0), (12, 2, 3), (12, 9, 0), (13, 2, 2),
    (16, 2, 1), (17, 2, 1), (16, 9, 0), (17, 9, 0), (13, 2, 3), (13, 9, 0),
)


def pick_positions(values, token_index):

    def pick_sequence(seq_values, seq_index):
        return jnp.take(seq_values, seq_index, axis=0)

    return jax.vmap(pick_sequence)(values, token_index)


def stack_rows(picked, query_side):
    width = picked.shape[-1]
    return jnp.concatenate([picked.reshape(-1, width), query_side.reshape(-1, width)], axis=0)


def project(row_data, basis_piece):
    return lax.dot_general(
        row_data, basis_piece, (((1,), (1,)), ((), ())), preferred_element_type=jnp.float32
    )


def make_scorer(own_rot, divisor, eigen, query_len, own_count, sel_count):
    score_scale = 1.0 / (eigen * math.sqrt(query_len))
    token_out = own_rot[:, :, :eigen].reshape(-1, eigen)
    token_in = own_rot[:, :, eigen:].reshape(-1, eigen)
    out_values = token_out.astype(jnp.float32)

    def score_query(query_item):
        rotated_query = lax.dot_general(
            query_item[:, :eigen],
            query_item[:, eigen:],
            (((0,), (0,)), ((), ())),
            preferred_element_type=jnp.float32,
        )
        precond = (rotated_query / divisor).astype(jnp.bfloat16)
        weighted = lax.dot_general(
            token_in, precond, (((1,), (1,)), ((), ())), preferred_element_type=jnp.float32
        )
        return jnp.sum(out_values * weighted, axis=1) * score_scale

    def score_block(pieces):
        values = lax.map(score_query, pieces, batch_size=16)
        return values.T.reshape(own_count, sel_count, pieces.shape[0])

    return score_block


def pick_damping(damp_table, layer_id):
    chosen = (jnp.arange(damp_table.shape[0], dtype=jnp.int32) == layer_id[0]).astype(jnp.float32)
    return jnp.sum(damp_table * chosen)


def local(
    train_grads,
    train_acts,
    token_index,
    query_grads,
    query_acts,
    out_basis,
    in_basis,
    corrections,
    damp_table,
    layer_id,
):
    grad_rows = stack_rows(pick_positions(train_grads, token_index), query_grads)
    act_rows = stack_rows(pick_positions(train_acts, token_index), query_acts)
    eigen = corrections.shape[1]
    pieces = (
        lax.all_gather(out_basis, "tok", axis=0, tiled=True),
        lax.all_gather(corrections, "tok", axis=0, tiled=True),
    )
    rot_out = project(grad_rows, pieces[0])
    corr_full = pieces[1]
    rot_in = project(act_rows, lax.all_gather(in_basis, "tok", axis=0, tiled=True))
    rotated = jnp.concatenate([rot_out, rot_in], axis=1)
    seq_count, sel_count = token_index.shape
    query_count, query_len = (query_grads.shape[0], query_grads.shape[1])
    train_part = rotated[: seq_count * sel_count].reshape(seq_count, sel_count, 2 * eigen)
    query_part = rotated[seq_count * sel_count :].reshape(query_count, query_len, 2 * eigen)
    own_count = seq_count // lax.axis_size("qry")
    divisor = corr_full.astype(jnp.float32) + pick_damping(damp_table, layer_id)
    train_sum, query_sum = lax.psum((train_part, query_part), "qry")
    own_train = lax.dynamic_slice_in_dim(train_sum, lax.axis_index("qry") * own_count, own_count, 0)
    scorer = make_scorer(
        own_train.astype(jnp.bfloat16), divisor, eigen, query_len, own_count, sel_count
    )
    return scorer(lax.all_gather(query_sum.astype(jnp.bfloat16), "tok", axis=0, tiled=True))


def rotate_kernel(
    out_ref,
    in_ref,
    own_corr_ref,
    query_grads_ref,
    query_acts_ref,
    grads_ref,
    acts_ref,
    rot_ref,
    query_ref,
    corr_ref,
    stack_ref,
    basis,
    rows,
    partner,
    acc,
    part_out,
    part_in,
    qpart_out,
    qpart_in,
    queries,
    own_sem,
    pair_send,
    pair_recv,
    up_send,
    down_send,
    z_recv,
    side_send,
    side_recv,
    query_send,
    query_recv,
):
    me = lax.axis_index("tok")
    core = lax.rem(me, 2)
    chip = me // 2
    x = lax.rem(me // 2, 2)
    y = lax.rem(me // 4, 2)
    z = me // 8
    nz = CHIPS[0]
    chips = nz * CHIPS[1] * CHIPS[2]
    sibling = me + 1 - 2 * core
    x_peer = me + 2 - 4 * x
    y_peer = me + 4 - 8 * y
    train, wide_out = grads_ref.shape
    half_out = wide_out // 2
    half_in = acts_ref.shape[1] // 2
    eigen = corr_ref.shape[1]
    chunk = (half_out + half_in) // len(KINDS)
    out_chunks = half_out // chunk

    def span(j):
        extra = eigen if j == len(KINDS) - 1 else 0
        return pl.ds(j * chunk, chunk + extra)

    def remote(src, dst, send, recv, device):
        return pltpu.make_async_remote_copy(
            src_ref=src,
            dst_ref=dst,
            send_sem=send,
            recv_sem=recv,
            device_id=(0, device, 0),
            device_id_type=pl.DeviceIdType.MESH,
        )

    own_copies = [
        pltpu.make_async_copy(
            grads_ref.at[:, pl.ds(core * half_out, half_out)],
            rows.at[pl.ds(0, train), pl.ds(0, half_out)],
            own_sem.at[0],
        ),
        pltpu.make_async_copy(
            acts_ref.at[:, pl.ds(core * half_in, half_in)],
            rows.at[pl.ds(0, train), pl.ds(half_out, half_in)],
            own_sem.at[1],
        ),
    ]
    for copy in own_copies:
        copy.start()

    def peer(s):
        return 2 * lax.rem(chip + s, chips) + core

    barrier = pltpu.get_barrier_semaphore()
    pl.semaphore_signal(
        barrier, inc=1, device_id=(0, sibling, 0), device_id_type=pl.DeviceIdType.MESH
    )

    def greet(s, carry):
        pl.semaphore_signal(
            barrier,
            inc=1,
            device_id=(0, peer(s), 0),
            device_id_type=pl.DeviceIdType.MESH,
        )
        return carry

    lax.fori_loop(1, chips, greet, 0)

    def pack(half, at, own, query, source, width):
        tops = own[:, pl.ds(source, width)].astype(jnp.float32)
        if query is None:
            ends = [jnp.zeros((8, width), jnp.float32)]
        else:
            ends = [
                query[q, :, pl.ds(source, width)].astype(jnp.float32)
                for q in range(query.shape[0])
            ]
        stack_ref[half, :, pl.ds(at, width)] = jnp.concatenate([tops, *ends], axis=0).astype(
            jnp.bfloat16
        )

    for half in range(2):
        for at in range(0, half_out, chunk):
            pack(half, at, out_ref, query_grads_ref, half * half_out + at, chunk)
        for at in range(0, half_in, chunk):
            pack(half, half_out + at, in_ref, query_acts_ref, half * half_in + at, chunk)
        pack(half, half_out + half_in, own_corr_ref, None, 0, eigen)
    pl.semaphore_wait(barrier, chips)

    early = EARLY * chunk
    stack_copies = [
        remote(
            stack_ref.at[1 - core, :, cols],
            partner.at[:, cols],
            pair_send.at[slot],
            pair_recv.at[slot],
            sibling,
        )
        for slot, cols in ((0, pl.ds(0, early)), (5, pl.ds(early, partner.shape[1] - early)))
    ]
    for copy in stack_copies:
        copy.start()
    row_copies = [
        remote(
            grads_ref.at[:, pl.ds((1 - core) * half_out, half_out)],
            rows.at[pl.ds(train, train), pl.ds(0, half_out)],
            pair_send.at[1],
            pair_recv.at[1],
            sibling,
        ),
        remote(
            acts_ref.at[:, pl.ds((1 - core) * half_in, half_in)],
            rows.at[pl.ds(train, train), pl.ds(half_out, half_in)],
            pair_send.at[2],
            pair_recv.at[2],
            sibling,
        ),
    ]
    for copy in row_copies:
        copy.start()
    acc[...] = jnp.zeros_like(acc)

    def build(j):
        cols = span(j)
        own = stack_ref[core, :, cols].astype(jnp.float32)
        other = partner[:, cols].astype(jnp.float32)
        first = jnp.where(core == 0, own, other)
        second = jnp.where(core == 0, other, own)
        basis[y, x, z, :, cols] = jnp.concatenate([first[:8], second[:8]], axis=0).astype(
            jnp.bfloat16
        )
        rows[pl.ds(2 * train, 16), cols] = jnp.concatenate(
            [first[8:], second[8:]], axis=0
        ).astype(jnp.bfloat16)

    def block(j, axis, at):
        before = KINDS[j][: KINDS[j].index(axis)]
        place = {"y": y, "x": x, "z": z, axis: at}
        index = [slice(None) if a in before else place[a] for a in "yxz"]
        return basis.at[(*index, slice(None), span(j))]

    def up_copy(j, source):
        ref = block(j, "z", source)
        return remote(ref, ref, up_send.at[j, source], z_recv.at[j, source], me + 8)

    def down_copy(j, source):
        ref = block(j, "z", source)
        return remote(ref, ref, down_send.at[j, source], z_recv.at[j, source], me - 8)

    def x_copy(j, at_x):
        ref = block(j, "x", at_x)
        return remote(ref, ref, side_send.at[0, j], side_recv.at[0, j], x_peer)

    def y_copy(j, at_y):
        ref = block(j, "y", at_y)
        return remote(ref, ref, side_send.at[1, j], side_recv.at[1, j], y_peer)

    def z_start(j):
        @pl.when(z < nz - 1)
        def _():
            up_copy(j, z).start()

        @pl.when(z > 0)
        def _():
            down_copy(j, z).start()

    def z_step(j, s):
        @pl.when(z - s >= 0)
        def _():
            up_copy(j, z - s).wait_recv()

            @pl.when(z < nz - 1)
            def _():
                up_copy(j, z - s).start()

        @pl.when(z + s < nz)
        def _():
            down_copy(j, z + s).wait_recv()

            @pl.when(z > 0)
            def _():
                down_copy(j, z + s).start()

    def x_start(j):
        x_copy(j, x).start()

    def y_start(j):
        y_copy(j, y).start()

    def x_wait(j):
        x_copy(j, 1 - x).wait_recv()

    def y_wait(j):
        y_copy(j, 1 - y).wait_recv()

    def natural(cols):
        return jnp.concatenate(
            [
                basis[b, a, c, :, cols]
                for c in range(nz)
                for b in range(CHIPS[1])
                for a in range(CHIPS[2])
            ],
            axis=0,
        )

    def compute(j):
        side = 0 if j < out_chunks else 1
        cols = pl.ds(j * chunk, chunk)
        acc[side] += lax.dot_general(
            rows[:, cols],
            natural(cols),
            (((1,), (1,)), ((), ())),
            preferred_element_type=jnp.float32,
        )

    last = len(KINDS) - 1
    starts = {"z": z_start, "x": x_start, "y": y_start}
    rows_here = False
    for j, place, step in ORDER:
        if place < 0:
            if j in (0, EARLY):
                stack_copies[j // EARLY].wait_recv()
            build(j)
            starts[KINDS[j][0]](j)
        elif place < len(KINDS[j]):
            axis = KINDS[j][place]
            if axis == "z":
                z_step(j, step)
            else:
                {"x": x_wait, "y": y_wait}[axis](j)
            if place + 1 < len(KINDS[j]) and (axis != "z" or step == nz - 1):
                starts[KINDS[j][place + 1]](j)
        else:
            if not rows_here:
                rows_here = True
                for copy in own_copies:
                    copy.wait()
                for copy in row_copies:
                    copy.wait_recv()
            compute(j)

    qpart_out[...] = acc[1 - core, pl.ds(2 * train, 16), :]
    qpart_copy = remote(qpart_out, qpart_in, pair_send.at[3], pair_recv.at[3], sibling)
    qpart_copy.start()
    part_out[...] = acc[:, pl.ds(train, train), :]
    part_copy = remote(part_out, part_in, pair_send.at[4], pair_recv.at[4], sibling)
    part_copy.start()
    qpart_copy.wait_recv()
    queries[core, chip] = (acc[core, pl.ds(2 * train, 16), :] + qpart_in[...]).astype(jnp.bfloat16)

    def query_copy(source, target):
        ref = queries.at[lax.rem(source, 2), source // 2]
        return remote(ref, ref, query_send.at[target], query_recv.at[source], target)

    def send_query(s, carry):
        query_copy(me, peer(s)).start()
        return carry

    lax.fori_loop(1, chips, send_query, 0)
    corr_ref[...] = natural(pl.ds(half_out + half_in, eigen))
    part_copy.wait_recv()
    rot_ref[...] = (acc[:, pl.ds(0, train), :] + part_in[...]).astype(jnp.bfloat16)

    for copy in stack_copies + row_copies:
        copy.wait_send()
    qpart_copy.wait_send()
    part_copy.wait_send()
    for j in range(last + 1):
        x_copy(j, x).wait_send()
        y_copy(j, y).wait_send()
        for s in range(nz):

            @pl.when(jnp.logical_and(z < nz - 1, z - s >= 0))
            def _():
                up_copy(j, z - s).wait_send()

            @pl.when(jnp.logical_and(z > 0, z + s < nz))
            def _():
                down_copy(j, z + s).wait_send()

    def wait_query(s, carry):
        source = peer(s)
        query_copy(source, source).wait_recv()
        return carry

    lax.fori_loop(1, chips, wait_query, 0)
    mine = queries.at[core]
    share = remote(mine, mine, pair_send.at[6], pair_recv.at[6], sibling)
    share.start()

    def finish_query(s, carry):
        query_copy(me, peer(s)).wait_send()
        return carry

    lax.fori_loop(1, chips, finish_query, 0)
    theirs = queries.at[1 - core]
    remote(theirs, theirs, pair_send.at[6], pair_recv.at[6], sibling).wait_recv()
    query_ref[...] = queries[...].reshape(query_ref.shape)
    share.wait_send()


def rotate_all(out_basis, in_basis, corrections, query_grads, query_acts, grads, acts):
    train, wide = grads.shape
    eigen = corrections.shape[1]
    total = (wide + acts.shape[1]) // 2 + eigen
    nz, ny, nx = CHIPS
    chips = nz * ny * nx
    n = len(KINDS)
    dma = pltpu.SemaphoreType.DMA
    vmem = pl.BlockSpec(memory_space=pltpu.VMEM)
    hbm = pl.BlockSpec(memory_space=pltpu.HBM)
    return pl.pallas_call(
        rotate_kernel,
        out_shape=(
            jax.ShapeDtypeStruct((2, train, eigen), jnp.bfloat16),
            jax.ShapeDtypeStruct((2, chips * 16, eigen), jnp.bfloat16),
            jax.ShapeDtypeStruct((eigen, eigen), jnp.bfloat16),
        ),
        in_specs=[vmem] * 5 + [hbm] * 2,
        out_specs=(vmem, vmem, vmem),
        scratch_shapes=[
            pltpu.VMEM((2, 16, total), jnp.bfloat16),
            pltpu.VMEM((ny, nx, nz, 16, total), jnp.bfloat16),
            pltpu.VMEM((2 * train + 16, total), jnp.bfloat16),
            pltpu.VMEM((16, total), jnp.bfloat16),
            pltpu.VMEM((2, 2 * train + 16, eigen), jnp.float32),
            pltpu.VMEM((2, train, eigen), jnp.float32),
            pltpu.VMEM((2, train, eigen), jnp.float32),
            pltpu.VMEM((16, eigen), jnp.float32),
            pltpu.VMEM((16, eigen), jnp.float32),
            pltpu.VMEM((2, chips, 16, eigen), jnp.bfloat16),
            dma((2,)),
            dma((7,)),
            dma((7,)),
            dma((n, nz)),
            dma((n, nz)),
            dma((n, nz)),
            dma((2, n)),
            dma((2, n)),
            dma((2 * chips,)),
            dma((2 * chips,)),
        ],
        compiler_params=pltpu.CompilerParams(
            collective_id=0, has_side_effects=True, vmem_limit_bytes=53 * 1024 * 1024
        ),
        cost_estimate=pl.CostEstimate(
            flops=4 * train * total * eigen, bytes_accessed=4 * train * wide, transcendentals=0
        ),
    )(out_basis, in_basis, corrections, query_grads, query_acts, grads, acts)


def local_fused(
    train_grads,
    train_acts,
    token_index,
    query_grads,
    query_acts,
    out_basis,
    in_basis,
    corrections,
    damp_table,
    layer_id,
):
    eigen = corrections.shape[1]
    seq_count, sel_count = token_index.shape
    length = train_grads.shape[1]
    query_len = query_grads.shape[1]
    wide_out, wide_in = out_basis.shape[1], in_basis.shape[1]
    rot, queries, corr = rotate_all(
        out_basis,
        in_basis,
        corrections,
        query_grads,
        query_acts,
        train_grads.reshape(-1, wide_out),
        train_acts.reshape(-1, wide_in),
    )
    one_hot = (token_index[:, :, None] == jnp.arange(length, dtype=token_index.dtype)).astype(
        jnp.bfloat16
    )
    positions = jnp.concatenate([rot[0], rot[1]], axis=1).reshape(seq_count, length, 2 * eigen)
    own_rot = jnp.einsum(
        "sjl,sle->sje", one_hot, positions, preferred_element_type=jnp.float32
    ).astype(jnp.bfloat16)
    divisor = corr.astype(jnp.float32) + pick_damping(damp_table, layer_id)
    scorer = make_scorer(own_rot, divisor, eigen, query_len, seq_count, sel_count)
    pieces = jnp.concatenate([queries[0], queries[1]], axis=1)
    return scorer(pieces.reshape(-1, query_len, 2 * eigen))


def solution(mesh):
    in_specs = (
        P(("layer", "tok"), None, "qry"),
        P(("layer", "tok"), None, "qry"),
        P("tok", None),
        P(("layer", "tok"), None, "qry"),
        P(("layer", "tok"), None, "qry"),
        P(("layer", "tok"), "qry"),
        P(("layer", "tok"), "qry"),
        P(("layer", "tok"), None),
        P(),
        P("layer"),
    )
    out_specs = P(("layer", "tok", "qry"), None, None)
    sizes = tuple(mesh.shape[axis] for axis in AXES)
    fused = sizes == (1, 2 * CHIPS[0] * CHIPS[1] * CHIPS[2], 1)
    return jax.shard_map(
        local_fused if fused else local,
        mesh=mesh,
        in_specs=in_specs,
        out_specs=out_specs,
        check_vma=False,
    )
```
